32 devices in a mesh: row: 8 (over y, x, core), col: 4 (over z).
Axes of the slice: x: 2, y: 2, z: 4, core: 2. Of those that a mesh axis runs over, the one named last changes fastest.
Arguments:
- users: float32 [8, 2048, 128], P('row', 'col'), may hold values from -2 to 2
- items: float32 [4096, 4, 128], P('row', 'col'), may hold values from -2 to 2
- block_user: int32 [8, 4, 48], P('row', 'col'), may hold values from 0 to 15
- block_item: int32 [8, 4, 48], P('row', 'col'), may hold values from 0 to 31
- ratings: bfloat16 [8, 4, 48, 128, 128], P('row', 'col'), may hold values from 0 to 5
- weights: bfloat16 [8, 4, 48, 128, 128], P('row', 'col'), may hold values from 0.099609375 to 3
Outputs:
- new_users: float32 [8, 2048, 128], P('row', 'col')
- new_items: float32 [4096, 4, 128], P('row', 'col')
The draws below stay inside these ranges and needn't reach their ends.
All inputs are finite; a program needn't handle non-finite values.
Results may differ from the reference program's by a relative error of at most 0.0021.
Values may be sent and summed in bfloat16 or wider, within the bound.
A program may use at most 64 MiB of HBM per device.

```python
import math
import jax
import jax.numpy as jnp
import numpy as np
from jax import lax

K = 128
BS = 128
NB = 48
UBR = 16
IBC = 32
USERS_ROW = 2048
ITEMS_COL = 4096
N_ROW = 8
N_COL = 4


def set_ends(array, stream_key, least, high):
    spot = [jax.random.randint(jax.random.fold_in(stream_key, axis), (), 0, length) for axis, length in enumerate(array.shape)]
    main_axis = array.shape.index(max(array.shape))
    next_to = spot[:main_axis] + [(spot[main_axis] + 1) % array.shape[main_axis]] + spot[main_axis + 1:]
    return array.at[tuple(spot)].set(least).at[tuple(next_to)].set(high)


def block_levels(key, dims, cuts, low, largest):
    loudness, own = 1.0, jax.random.fold_in(key, 6)
    for axis_at, shards_of in cuts:
        steps = jnp.exp(jax.random.uniform(jax.random.fold_in(own, axis_at), (shards_of,), jnp.float32, low / len(cuts), largest / len(cuts)))
        loudness = loudness * jnp.repeat(steps, dims[axis_at] // shards_of).reshape([-1 if axis == axis_at else 1 for axis in range(len(dims))])
    return loudness


def rank_table(count, lean):
    portions = [(1 << 20) // math.isqrt(standing ** lean) + 1 for standing in range(1, count + 1)]
    spread = 1 + sum(portions) // (1 << 30)
    return np.cumsum(np.array([max(1, weight // spread) for weight in portions]))


def ranked(stream_key, shape, count, lean):
    table = rank_table(count, lean)
    ticket = jax.random.randint(jax.random.fold_in(stream_key, 1), shape, 0, int(table[count - 1]))
    grade = jnp.searchsorted(jnp.asarray(table, jnp.int32), ticket, side="right")
    return jax.random.permutation(jax.random.fold_in(stream_key, 2), count)[grade].astype(jnp.int32)


def centred(rng, dims, deviation, limit, split=(), kind=jnp.bfloat16):
    values = jax.random.normal(rng, dims, jnp.float32) * deviation
    if len(split) > 0:
        values = block_levels(rng, dims, split, -0.22, 0.18) * values
    return jnp.clip(values, min=-limit, max=limit).astype(kind)


def setup_inputs(seed: int = 0) -> dict:
    key_of = jax.random.split(jax.random.key(seed), 7)
    return {
        "users": centred(key_of[0], (N_ROW, USERS_ROW, K), 0.3, 2.0, ((0, 8), (1, 4)), jnp.float32),
        "items": centred(key_of[1], (ITEMS_COL, N_COL, K), 0.3, 2.0, ((0, 8), (1, 4)), jnp.float32),
        "block_user": set_ends(jax.random.randint(key_of[2], (N_ROW, N_COL, NB), 0, UBR), jax.random.fold_in(key_of[2], 1), 0, UBR - 1).astype(jnp.int32),
        "block_item": set_ends(ranked(key_of[3], (N_ROW, N_COL, NB), IBC, 2), jax.random.fold_in(key_of[3], 3), 0, IBC - 1).astype(jnp.int32),
        "ratings": jnp.clip(5.0 * jax.random.uniform(key_of[4], (N_ROW, N_COL, NB, BS, BS), jnp.float32) ** block_levels(key_of[4], (N_ROW, N_COL, NB, BS, BS), ((0, 8), (1, 4)), -0.2, 0.2), 0.0, 5.0).astype(jnp.bfloat16),
        "weights": jnp.clip(jnp.exp(math.log(3.0) - 3.4051113 * jax.random.uniform(key_of[5], (N_ROW, N_COL, NB, BS, BS), jnp.float32) ** block_levels(key_of[5], (N_ROW, N_COL, NB, BS, BS), ((0, 8), (1, 4)), -0.2, 0.2)), 0.099609375, 3.0).astype(jnp.bfloat16),
    }


def cell_grads(user_slab, item_slab, bu, bi, rating_tiles, weight_tiles):
    ub = jnp.take(user_slab, bu, axis=0).astype(jnp.float32)
    vb = jnp.take(item_slab, bi, axis=0).astype(jnp.float32)
    pred = jnp.einsum('bik,bjk->bij', ub, vb)
    wts = weight_tiles.astype(jnp.float32)
    resid = (wts * (pred - rating_tiles.astype(jnp.float32))).astype(jnp.bfloat16).astype(jnp.float32)
    ugb = jnp.einsum('bij,bjk->bik', resid, vb)
    vgb = jnp.einsum('bij,bik->bjk', resid, ub)
    uhot = (bu[:, None] == jnp.arange(user_slab.shape[0], dtype=jnp.int32)[None, :]).astype(jnp.float32)
    vhot = (bi[:, None] == jnp.arange(item_slab.shape[0], dtype=jnp.int32)[None, :]).astype(jnp.float32)
    hi = lax.Precision.HIGHEST
    ugrad = jnp.einsum('bu,bik->uik', uhot, ugb, precision=hi)
    vgrad = jnp.einsum('bv,bjk->vjk', vhot, vgb, precision=hi)
    usum = jnp.einsum('bu,bi->ui', uhot, jnp.sum(wts, axis=2), precision=hi)
    vsum = jnp.einsum('bv,bj->vj', vhot, jnp.sum(wts, axis=1), precision=hi)
    return ugrad, usum, vgrad, vsum


def reference(users, items, block_user, block_item, ratings, weights):
    user_low = users.astype(jnp.bfloat16).reshape(N_ROW, UBR, BS, K)
    item_low = items.astype(jnp.bfloat16).reshape(IBC, BS, N_COL, K)
    user_grad = jnp.zeros((N_ROW, UBR, BS, K), jnp.float32)
    user_wsum = jnp.zeros((N_ROW, UBR, BS), jnp.float32)
    item_grad = jnp.zeros((N_COL, IBC, BS, K), jnp.float32)
    item_wsum = jnp.zeros((N_COL, IBC, BS), jnp.float32)

    def step(carry, cell):
        ug, us, vg, vs = carry
        rindex = (cell // N_COL).astype(jnp.int32)
        cindex = (cell % N_COL).astype(jnp.int32)
        uslab = lax.dynamic_index_in_dim(user_low, rindex, 0, keepdims=False)
        vslab = lax.dynamic_index_in_dim(item_low, cindex, 2, keepdims=False)
        bu = block_user[rindex, cindex]
        bi = block_item[rindex, cindex]
        rt = ratings[rindex, cindex]
        wt = weights[rindex, cindex]
        a, b, c, d = cell_grads(uslab, vslab, bu, bi, rt, wt)
        ug = ug.at[rindex].add(a)
        us = us.at[rindex].add(b)
        vg = vg.at[cindex].add(c)
        vs = vs.at[cindex].add(d)
        return (ug, us, vg, vs), None

    cells = jnp.arange(N_ROW * N_COL, dtype=jnp.int32)
    (user_grad, user_wsum, item_grad, item_wsum), _ = lax.scan(step, (user_grad, user_wsum, item_grad, item_wsum), cells)
    ug = user_grad.reshape(N_ROW, UBR * BS, K)
    us = user_wsum.reshape(N_ROW, UBR * BS, 1)
    new_users = users - 2.0 * (ug + 0.5 * users) / (1.0 + us)
    vg = jnp.transpose(item_grad.reshape(N_COL, IBC * BS, K), (1, 0, 2))
    vs = jnp.transpose(item_wsum.reshape(N_COL, IBC * BS, 1), (1, 0, 2))
    new_items = items - 2.0 * (vg + 0.5 * items) / (1.0 + vs)
    return new_users, new_items
```

```python
import functools

import jax
import jax.numpy as jnp
from jax import lax
from jax.experimental import pallas as pl
from jax.experimental.pallas import tpu as pltpu
from jax.sharding import PartitionSpec as P

BS = 128
MESH = pl.DeviceIdType.MESH
NT = (((1,), (1,)), ((), ()))
NN = (((1,), (0,)), ((), ()))
TN = (((0,), (0,)), ((), ()))


def dot(a, b, dims):
    return lax.dot_general(a, b, dims, preferred_element_type=jnp.float32)


def chain_tables(key_ref, pad_ref, count):
    pad_ref[...] = jnp.full((8, 128), -1, jnp.int32)
    pad_ref[0:1, 0:count] = key_ref[...]
    across = jnp.broadcast_to(pad_ref[0:1, :], (128, 128))
    down = across.T
    i = lax.broadcasted_iota(jnp.int32, (128, 128), 0)
    j = lax.broadcasted_iota(jnp.int32, (128, 128), 1)
    prev = jnp.max(jnp.where((down == across) & (i < j), i + 1, 0), axis=0, keepdims=True)
    last = jnp.max(jnp.where(down == j, i + 1, 0), axis=0, keepdims=True)
    return prev, last, jnp.maximum(pad_ref[0:1, :], 0)


def spots(index, own):
    if own >= BS:
        blocks = own // BS
        return [(index * blocks + k, 0, BS) for k in range(blocks)]
    per = BS // own
    return [(lax.div(index, per), lax.rem(index, per) * own, own)]


def part(block, first, rows, turn_ref):
    if rows == BS:
        return block
    turn_ref[...] = block
    return turn_ref[pl.ds(pl.multiple_of(first, rows), rows), :]


def owned(slab_ref, index, own):
    if own >= BS:
        return slab_ref.at[pl.ds(index * (own // BS), own // BS)]
    per = BS // own
    return slab_ref.at[lax.div(index, per), pl.ds(pl.multiple_of(lax.rem(index, per) * own, own), own)]


def weight_tile(wseg_ref, slots):
    row = lax.broadcasted_iota(jnp.int32, (8, 128), 0)
    tile = jnp.zeros((8, 128), jnp.float32)
    for k, slot in enumerate(slots):
        tile = jnp.where(row == k, wseg_ref[slot], tile)
    return tile


def pack(seg_ref, wseg_ref, tab, line, index, own, out_ref, place, turn_ref):
    pieces = spots(index, own)
    slots = [tab[line, block] for block, _, _ in pieces]
    for k, (slot, (_, first, rows)) in enumerate(zip(slots, pieces)):
        out_ref[place, k * BS : k * BS + rows, :] = part(seg_ref[slot], first, rows, turn_ref).astype(jnp.bfloat16)
    tile = weight_tile(wseg_ref, slots)
    high = tile.astype(jnp.bfloat16).astype(jnp.float32)
    both = jnp.concatenate([high, tile - high], axis=0)
    out_ref[place, own : own + 16, :] = both.astype(jnp.bfloat16)


def update(old_ref, seg_ref, wseg_ref, tab, line, index, own, recv_ref, waits, acc_ref, turn_ref, new_ref):
    pieces = spots(index, own)
    slots = [tab[line, block] for block, _, _ in pieces]
    for k, (slot, (_, first, rows)) in enumerate(zip(slots, pieces)):
        acc_ref[k * BS : k * BS + rows, :] = part(seg_ref[slot], first, rows, turn_ref)
    tile = weight_tile(wseg_ref, slots)
    for place, wait in enumerate(waits):
        wait()
        acc_ref[...] += recv_ref[place, 0:own, :].astype(jnp.float32)
        both = recv_ref[place, own : own + 16, :].astype(jnp.float32)
        tile = tile + (both[0:8] + both[8:16])
    for k, (_, first, rows) in enumerate(pieces):
        turned = jnp.broadcast_to(tile[k : k + 1, :], (BS, BS)).T
        turned = part(turned, first, rows, turn_ref)
        at = slice(k * BS, k * BS + rows)
        old = old_ref[at, :]
        new_ref[at, :] = old - 2.0 * (acc_ref[at, :] + 0.5 * old) / (1.0 + turned)


def kernel(
    n_row, n_col, count, own_u, own_i,
    users, items, bu, bi, ratings, weights,
    new_users, new_items,
    slab_u, slab_i, rat, wts, resid, seg_u, seg_i, wseg_u, wseg_i,
    send_u, send_i, recv_u, recv_i, acc_u, acc_i, turn, pad, tab_v, tab,
    load_sem, gu_send, gu_recv, gi_send, gi_recv, ru_send, ru_recv, ri_send, ri_recv,
):
    row, col = lax.axis_index("row"), lax.axis_index("col")
    col_peers = [lax.rem(col + d, n_col) for d in range(1, n_col)]
    row_peers = [lax.rem(row + d, n_row) for d in range(1, n_row)]

    barrier = pltpu.get_barrier_semaphore()
    for peer in col_peers:
        pl.semaphore_signal(barrier, inc=1, device_id=(row, peer), device_id_type=MESH)
    for peer in row_peers:
        pl.semaphore_signal(barrier, inc=1, device_id=(peer, col), device_id_type=MESH)
    load_rat = pltpu.make_async_copy(ratings, rat, load_sem.at[0])
    load_wts = pltpu.make_async_copy(weights, wts, load_sem.at[1])
    load_rat.start()
    load_wts.start()
    mine_u, mine_i = owned(slab_u, col, own_u), owned(slab_i, row, own_i)
    mine_u[...] = users[...].astype(jnp.bfloat16).reshape(mine_u.shape)
    mine_i[...] = items[...].astype(jnp.bfloat16).reshape(mine_i.shape)
    pl.semaphore_wait(barrier, n_col + n_row - 2)

    gathers = []
    for place, peer in enumerate(col_peers):
        gathers.append(pltpu.make_async_remote_copy(
            src_ref=mine_u, dst_ref=mine_u,
            send_sem=gu_send.at[place], recv_sem=gu_recv.at[place],
            device_id=(row, peer), device_id_type=MESH))
    for place, peer in enumerate(row_peers):
        gathers.append(pltpu.make_async_remote_copy(
            src_ref=mine_i, dst_ref=mine_i,
            send_sem=gi_send.at[place], recv_sem=gi_recv.at[place],
            device_id=(peer, col), device_id_type=MESH))
    for copy in gathers:
        copy.start()

    prev_u, last_u, key_u = chain_tables(bu, pad, count)
    prev_i, last_i, key_i = chain_tables(bi, pad, count)
    for line, values in enumerate((prev_u, prev_i, last_u, last_i, key_u, key_i)):
        tab_v[line : line + 1, :] = values
    to_scalar = pltpu.make_async_copy(tab_v, tab, load_sem.at[2])
    to_scalar.start()
    seg_u[0] = jnp.zeros((BS, BS), jnp.float32)
    seg_i[0] = jnp.zeros((BS, BS), jnp.float32)
    wseg_u[0] = jnp.zeros((8, BS), jnp.float32)
    wseg_i[0] = jnp.zeros((8, BS), jnp.float32)
    to_scalar.wait()
    load_rat.wait()
    load_wts.wait()

    ones = jnp.ones((8, BS), jnp.bfloat16)

    def weight_step(b, carry):
        w = wts[b]
        wseg_u[b + 1] = wseg_u[tab[0, b]] + dot(ones, w, NT)
        wseg_i[b + 1] = wseg_i[tab[1, b]] + dot(ones, w, NN)
        return carry

    lax.fori_loop(0, count, weight_step, 0, unroll=4)

    for copy in gathers:
        copy.wait()

    def user_step(b, carry):
        u = slab_u[tab[4, b]]
        v = slab_i[tab[5, b]]
        pred = dot(u, v, NT)
        r = (wts[b].astype(jnp.float32) * (pred - rat[b].astype(jnp.float32))).astype(jnp.bfloat16)
        resid[b] = r
        seg_u[b + 1] = seg_u[tab[0, b]] + dot(r, v, NN)
        return carry

    lax.fori_loop(0, count, user_step, 0, unroll=4)

    sends_u = []
    for place, peer in enumerate(col_peers):
        pack(seg_u, wseg_u, tab, 2, peer, own_u, send_u, place, turn)
        copy = pltpu.make_async_remote_copy(
            src_ref=send_u.at[place], dst_ref=recv_u.at[place],
            send_sem=ru_send.at[place], recv_sem=ru_recv.at[place],
            device_id=(row, peer), device_id_type=MESH)
        copy.start()
        sends_u.append(copy)

    def item_step(b, carry):
        u = slab_u[tab[4, b]]
        seg_i[b + 1] = seg_i[tab[1, b]] + dot(resid[b], u, TN)
        return carry

    lax.fori_loop(0, count, item_step, 0, unroll=4)

    sends_i = []
    for place, peer in enumerate(row_peers):
        pack(seg_i, wseg_i, tab, 3, peer, own_i, send_i, place, turn)
        copy = pltpu.make_async_remote_copy(
            src_ref=send_i.at[place], dst_ref=recv_i.at[place],
            send_sem=ri_send.at[place], recv_sem=ri_recv.at[place],
            device_id=(peer, col), device_id_type=MESH)
        copy.start()
        sends_i.append(copy)

    update(users, seg_u, wseg_u, tab, 2, col, own_u, recv_u, [c.wait_recv for c in sends_u], acc_u, turn, new_users)
    update(items, seg_i, wseg_i, tab, 3, row, own_i, recv_i, [c.wait_recv for c in sends_i], acc_i, turn, new_items)
    for copy in sends_u + sends_i:
        copy.wait_send()


def shards(n_row, n_col, users, items, block_user, block_item, ratings, weights):
    own_u, own_i = users.shape[1], items.shape[0]
    width = users.shape[2]
    count = block_user.shape[2]
    all_u, all_i = own_u * n_col, own_i * n_row
    vmem = pl.BlockSpec(memory_space=pltpu.VMEM)
    hbm = pl.BlockSpec(memory_space=pl.ANY)
    bf16, f32, i32 = jnp.bfloat16, jnp.float32, jnp.int32
    dma = pltpu.SemaphoreType.DMA
    new_users, new_items = pl.pallas_call(
        functools.partial(kernel, n_row, n_col, count, own_u, own_i),
        out_shape=(
            jax.ShapeDtypeStruct((own_u, width), f32),
            jax.ShapeDtypeStruct((own_i, width), f32),
        ),
        in_specs=[vmem, vmem, vmem, vmem, hbm, hbm],
        out_specs=(vmem, vmem),
        scratch_shapes=[
            pltpu.VMEM((all_u // BS, BS, width), bf16),
            pltpu.VMEM((all_i // BS, BS, width), bf16),
            pltpu.VMEM((count, BS, BS), bf16),
            pltpu.VMEM((count, BS, BS), bf16),
            pltpu.VMEM((count, BS, BS), bf16),
            pltpu.VMEM((count + 1, BS, width), f32),
            pltpu.VMEM((count + 1, BS, width), f32),
            pltpu.VMEM((count + 1, 8, BS), f32),
            pltpu.VMEM((count + 1, 8, BS), f32),
            pltpu.VMEM((n_col - 1, own_u + 16, width), bf16),
            pltpu.VMEM((n_row - 1, own_i + 16, width), bf16),
            pltpu.VMEM((n_col - 1, own_u + 16, width), bf16),
            pltpu.VMEM((n_row - 1, own_i + 16, width), bf16),
            pltpu.VMEM((own_u, width), f32),
            pltpu.VMEM((own_i, width), f32),
            pltpu.VMEM((BS, BS), f32),
            pltpu.VMEM((8, 128), i32),
            pltpu.VMEM((8, 128), i32),
            pltpu.SMEM((8, 128), i32),
            dma((3,)),
            dma((n_col - 1,)),
            dma((n_col - 1,)),
            dma((n_row - 1,)),
            dma((n_row - 1,)),
            dma((n_col - 1,)),
            dma((n_col - 1,)),
            dma((n_row - 1,)),
            dma((n_row - 1,)),
        ],
        compiler_params=pltpu.CompilerParams(
            collective_id=0, has_side_effects=True, vmem_limit_bytes=40 << 20
        ),
        cost_estimate=pl.CostEstimate(
            flops=6 * count * BS * BS * width, bytes_accessed=4 * count * BS * BS, transcendentals=0
        ),
    )(
        users.reshape(own_u, width),
        items.reshape(own_i, width),
        block_user.reshape(1, count),
        block_item.reshape(1, count),
        ratings.reshape(count, BS, BS),
        weights.reshape(count, BS, BS),
    )
    return (new_users.reshape(users.shape), new_items.reshape(items.shape))


def solution(mesh):
    sizes = dict(mesh.shape)
    return jax.shard_map(
        functools.partial(shards, sizes["row"], sizes["col"]),
        mesh=mesh,
        in_specs=(
            P("row", "col", None),
            P("row", "col", None),
            P("row", "col", None),
            P("row", "col", None),
            P("row", "col", None, None, None),
            P("row", "col", None, None, None),
        ),
        out_specs=(P("row", "col", None), P("row", "col", None)),
        check_vma=False,
    )
```

```python
import functools

import jax
import jax.numpy as jnp
from jax import lax
from jax.experimental import pallas as pl
from jax.experimental.pallas import tpu as pltpu
from jax.sharding import PartitionSpec as P

BS = 128
GROUP = 8
MESH = pl.DeviceIdType.MESH
NT = (((1,), (1,)), ((), ()))
NN = (((1,), (0,)), ((), ()))
TN = (((0,), (0,)), ((), ()))


def dot(a, b, dims):
    return lax.dot_general(a, b, dims, preferred_element_type=jnp.float32)


def chain_tables(key_ref, pad_ref, count):
    pad_ref[...] = jnp.full((8, 128), -1, jnp.int32)
    pad_ref[0:1, 0:count] = key_ref[...]
    across = jnp.broadcast_to(pad_ref[0:1, :], (128, 128))
    down = across.T
    i = lax.broadcasted_iota(jnp.int32, (128, 128), 0)
    j = lax.broadcasted_iota(jnp.int32, (128, 128), 1)
    prev = jnp.max(jnp.where((down == across) & (i < j), i + 1, 0), axis=0, keepdims=True)
    last = jnp.max(jnp.where(down == j, i + 1, 0), axis=0, keepdims=True)
    return prev, last, jnp.maximum(pad_ref[0:1, :], 0)


def spots(index, own):
    if own >= BS:
        blocks = own // BS
        return [(index * blocks + k, 0, BS) for k in range(blocks)]
    per = BS // own
    return [(lax.div(index, per), lax.rem(index, per) * own, own)]


def part(block, first, rows, turn_ref):
    if rows == BS:
        return block
    turn_ref[...] = block
    return turn_ref[pl.ds(pl.multiple_of(first, rows), rows), :]


def owned(slab_ref, index, own):
    if own >= BS:
        return slab_ref.at[pl.ds(index * (own // BS), own // BS)]
    per = BS // own
    return slab_ref.at[lax.div(index, per), pl.ds(pl.multiple_of(lax.rem(index, per) * own, own), own)]


def weight_tile(wseg_ref, slots):
    row = lax.broadcasted_iota(jnp.int32, (8, 128), 0)
    tile = jnp.zeros((8, 128), jnp.float32)
    for k, slot in enumerate(slots):
        tile = jnp.where(row == k, wseg_ref[slot], tile)
    return tile


def weight_sums(ref, place, own):
    both = ref[place, own : own + 16, :].astype(jnp.float32)
    return both[0:8] + both[8:16]


def pack(seg_ref, wseg_ref, tab, line, index, own, out_ref, place, turn_ref, held_ref=None, held=None):
    pieces = spots(index, own)
    slots = [tab[line, block] for block, _, _ in pieces]
    for k, (slot, (_, first, rows)) in enumerate(zip(slots, pieces)):
        at = slice(k * BS, k * BS + rows)
        sums = part(seg_ref[slot], first, rows, turn_ref)
        if held_ref is not None:
            sums = sums + held_ref[held, at, :].astype(jnp.float32)
        out_ref[place, at, :] = sums.astype(jnp.bfloat16)
    tile = weight_tile(wseg_ref, slots)
    if held_ref is not None:
        tile = tile + weight_sums(held_ref, held, own)
    high = tile.astype(jnp.bfloat16).astype(jnp.float32)
    both = jnp.concatenate([high, tile - high], axis=0)
    out_ref[place, own : own + 16, :] = both.astype(jnp.bfloat16)


def update(old_ref, seg_ref, wseg_ref, tab, line, index, own, terms, acc_ref, turn_ref, new_ref):
    pieces = spots(index, own)
    slots = [tab[line, block] for block, _, _ in pieces]
    for k, (slot, (_, first, rows)) in enumerate(zip(slots, pieces)):
        acc_ref[k * BS : k * BS + rows, :] = part(seg_ref[slot], first, rows, turn_ref)
    tile = weight_tile(wseg_ref, slots)
    for wait, recv_ref, place in terms:
        wait()
        acc_ref[...] += recv_ref[place, 0:own, :].astype(jnp.float32)
        tile = tile + weight_sums(recv_ref, place, own)
    for k, (_, first, rows) in enumerate(pieces):
        turned = jnp.broadcast_to(tile[k : k + 1, :], (BS, BS)).T
        turned = part(turned, first, rows, turn_ref)
        at = slice(k * BS, k * BS + rows)
        old = old_ref[at, :]
        new_ref[at, :] = old - 2.0 * (acc_ref[at, :] + 0.5 * old) / (1.0 + turned)


def kernel(
    n_row, n_col, count, own_u, own_i,
    users_hbm, items_hbm, bu_hbm, bi_hbm, ratings, weights,
    new_users, new_items,
    users, items, bu, bi,
    slab_u, slab_i, rat, wts, resid, seg_u, seg_i, wseg_u, wseg_i,
    send_u, send_t, send_i, recv_u, recv_t, recv_i, acc_u, acc_i, turn, pad, tab_v, tab,
    load_sem, gu_send, gu_recv, gi_send, gi_recv, gf_send, gf_recv,
    ru_send, ru_recv, rt_send, rt_recv, ri_send, ri_recv,
):
    row, col = lax.axis_index("row"), lax.axis_index("col")
    col_peers = [lax.rem(col + d, n_col) for d in range(1, n_col)]
    twin = row + 1 - 2 * lax.rem(row, 2)
    half = n_row // 2
    row_peers = [lax.rem(row + 2 * d, n_row) for d in range(1, half)]

    barrier = pltpu.get_barrier_semaphore()
    for peer in col_peers:
        pl.semaphore_signal(barrier, inc=1, device_id=(row, peer), device_id_type=MESH)
    for peer in row_peers + [twin]:
        pl.semaphore_signal(barrier, inc=1, device_id=(peer, col), device_id_type=MESH)
    sources = (users_hbm, items_hbm, bu_hbm, bi_hbm, weights, ratings)
    loads = [
        pltpu.make_async_copy(source, place, load_sem.at[k])
        for k, (source, place) in enumerate(zip(sources, (users, items, bu, bi, wts, rat)))
    ]
    for load in loads:
        load.start()
    load_wts, load_rat = loads[4:]
    for load in loads[:4]:
        load.wait()
    mine_u, mine_i = owned(slab_u, col, own_u), owned(slab_i, row, own_i)
    mine_u[...] = users[...].astype(jnp.bfloat16).reshape(mine_u.shape)
    mine_i[...] = items[...].astype(jnp.bfloat16).reshape(mine_i.shape)
    pl.semaphore_wait(barrier, n_col + half - 1)

    gathers = []
    for place, peer in enumerate(col_peers):
        gathers.append(pltpu.make_async_remote_copy(
            src_ref=mine_u, dst_ref=mine_u,
            send_sem=gu_send.at[place], recv_sem=gu_recv.at[place],
            device_id=(row, peer), device_id_type=MESH))
    for place, peer in enumerate(row_peers + [twin]):
        gathers.append(pltpu.make_async_remote_copy(
            src_ref=mine_i, dst_ref=mine_i,
            send_sem=gi_send.at[place], recv_sem=gi_recv.at[place],
            device_id=(peer, col), device_id_type=MESH))
    for copy in gathers:
        copy.start()

    prev_u, last_u, key_u = chain_tables(bu, pad, count)
    prev_i, last_i, key_i = chain_tables(bi, pad, count)
    for line, values in enumerate((prev_u, prev_i, last_u, last_i, key_u, key_i)):
        tab_v[line : line + 1, :] = values
    to_scalar = pltpu.make_async_copy(tab_v, tab, load_sem.at[6])
    to_scalar.start()
    seg_u[0] = jnp.zeros((BS, BS), jnp.float32)
    seg_i[0] = jnp.zeros((BS, BS), jnp.float32)
    wseg_u[0] = jnp.zeros((8, BS), jnp.float32)
    wseg_i[0] = jnp.zeros((8, BS), jnp.float32)
    to_scalar.wait()
    load_wts.wait()

    ones = jnp.ones((8, BS), jnp.bfloat16)

    def weight_step(b, carry):
        w = wts[b]
        wseg_u[b + 1] = wseg_u[tab[0, b]] + dot(ones, w, NT)
        wseg_i[b + 1] = wseg_i[tab[1, b]] + dot(ones, w, NN)
        return carry

    lax.fori_loop(0, count, weight_step, 0, unroll=4)

    load_rat.wait()
    forwards = []
    for place in range(half - 1):
        gathers[n_col - 1 + place].wait_recv()
        block = owned(slab_i, lax.rem(row + n_row - 2 * (place + 1), n_row), own_i)
        copy = pltpu.make_async_remote_copy(
            src_ref=block, dst_ref=block, send_sem=gf_send.at[place], recv_sem=gf_recv.at[place],
            device_id=(twin, col), device_id_type=MESH)
        copy.start()
        forwards.append(copy)
    for k, copy in enumerate(gathers):
        copy.wait_send()
        if k < n_col - 1 or k == len(gathers) - 1:
            copy.wait_recv()
    for copy in forwards:
        copy.wait()

    group = GROUP if count % GROUP == 0 else 1

    def user_step(g, carry):
        blocks = [g * group + k for k in range(group)]
        us = [slab_u[tab[4, b]] for b in blocks]
        vs = [slab_i[tab[5, b]] for b in blocks]
        preds = [dot(u, v, NT) for u, v in zip(us, vs)]
        rs = [
            (wts[b].astype(jnp.float32) * (pred - rat[b].astype(jnp.float32))).astype(jnp.bfloat16)
            for b, pred in zip(blocks, preds)
        ]
        grads = [dot(r, v, NN) for r, v in zip(rs, vs)]
        for b, r in zip(blocks, rs):
            resid[b] = r
        for b, grad in zip(blocks, grads):
            seg_u[b + 1] = seg_u[tab[0, b]] + grad
        return carry

    lax.fori_loop(0, count // group, user_step, 0)

    sends_u = []
    for place, peer in enumerate(col_peers):
        pack(seg_u, wseg_u, tab, 2, peer, own_u, send_u, place, turn)
        copy = pltpu.make_async_remote_copy(
            src_ref=send_u.at[place], dst_ref=recv_u.at[place],
            send_sem=ru_send.at[place], recv_sem=ru_recv.at[place],
            device_id=(row, peer), device_id_type=MESH)
        copy.start()
        sends_u.append(copy)

    def item_step(b, carry):
        u = slab_u[tab[4, b]]
        seg_i[b + 1] = seg_i[tab[1, b]] + dot(resid[b], u, TN)
        return carry

    lax.fori_loop(0, count, item_step, 0, unroll=4)

    to_twin = []
    for place in list(range(1, half)) + [0]:
        pack(seg_i, wseg_i, tab, 3, lax.rem(twin + 2 * place, n_row), own_i, send_t, place, turn)
        copy = pltpu.make_async_remote_copy(
            src_ref=send_t.at[place], dst_ref=recv_t.at[place],
            send_sem=rt_send.at[place], recv_sem=rt_recv.at[place],
            device_id=(twin, col), device_id_type=MESH)
        copy.start()
        to_twin.append(copy)

    sends_i = []
    for place, peer in enumerate(row_peers):
        to_twin[place].wait_recv()
        pack(seg_i, wseg_i, tab, 3, peer, own_i, send_i, place, turn, recv_t, place + 1)
        copy = pltpu.make_async_remote_copy(
            src_ref=send_i.at[place], dst_ref=recv_i.at[place],
            send_sem=ri_send.at[place], recv_sem=ri_recv.at[place],
            device_id=(peer, col), device_id_type=MESH)
        copy.start()
        sends_i.append(copy)

    terms_u = [(c.wait_recv, recv_u, k) for k, c in enumerate(sends_u)]
    terms_i = [(to_twin[-1].wait_recv, recv_t, 0)] + [(c.wait_recv, recv_i, k) for k, c in enumerate(sends_i)]
    update(users, seg_u, wseg_u, tab, 2, col, own_u, terms_u, acc_u, turn, new_users)
    update(items, seg_i, wseg_i, tab, 3, row, own_i, terms_i, acc_i, turn, new_items)
    for copy in sends_u + to_twin + sends_i:
        copy.wait_send()


def shards(n_row, n_col, users, items, block_user, block_item, ratings, weights):
    own_u, own_i = users.shape[1], items.shape[0]
    width = users.shape[2]
    count = block_user.shape[2]
    half = n_row // 2
    all_u, all_i = own_u * n_col, own_i * n_row
    vmem = pl.BlockSpec(memory_space=pltpu.VMEM)
    hbm = pl.BlockSpec(memory_space=pl.ANY)
    bf16, f32, i32 = jnp.bfloat16, jnp.float32, jnp.int32
    dma = pltpu.SemaphoreType.DMA
    new_users, new_items = pl.pallas_call(
        functools.partial(kernel, n_row, n_col, count, own_u, own_i),
        out_shape=(
            jax.ShapeDtypeStruct((own_u, width), f32),
            jax.ShapeDtypeStruct((own_i, width), f32),
        ),
        in_specs=[hbm] * 6,
        out_specs=(vmem, vmem),
        scratch_shapes=[
            pltpu.VMEM((own_u, width), f32),
            pltpu.VMEM((own_i, width), f32),
            pltpu.VMEM((1, count), i32),
            pltpu.VMEM((1, count), i32),
            pltpu.VMEM((all_u // BS, BS, width), bf16),
            pltpu.VMEM((all_i // BS, BS, width), bf16),
            pltpu.VMEM((count, BS, BS), bf16),
            pltpu.VMEM((count, BS, BS), bf16),
            pltpu.VMEM((count, BS, BS), bf16),
            pltpu.VMEM((count + 1, BS, width), f32),
            pltpu.VMEM((count + 1, BS, width), f32),
            pltpu.VMEM((count + 1, 8, BS), f32),
            pltpu.VMEM((count + 1, 8, BS), f32),
            pltpu.VMEM((n_col - 1, own_u + 16, width), bf16),
            pltpu.VMEM((half, own_i + 16, width), bf16),
            pltpu.VMEM((half - 1, own_i + 16, width), bf16),
            pltpu.VMEM((n_col - 1, own_u + 16, width), bf16),
            pltpu.VMEM((half, own_i + 16, width), bf16),
            pltpu.VMEM((half - 1, own_i + 16, width), bf16),
            pltpu.VMEM((own_u, width), f32),
            pltpu.VMEM((own_i, width), f32),
            pltpu.VMEM((BS, BS), f32),
            pltpu.VMEM((8, 128), i32),
            pltpu.VMEM((8, 128), i32),
            pltpu.SMEM((8, 128), i32),
            dma((7,)),
            dma((n_col - 1,)),
            dma((n_col - 1,)),
            dma((half,)),
            dma((half,)),
            dma((half - 1,)),
            dma((half - 1,)),
            dma((n_col - 1,)),
            dma((n_col - 1,)),
            dma((half,)),
            dma((half,)),
            dma((half - 1,)),
            dma((half - 1,)),
        ],
        compiler_params=pltpu.CompilerParams(
            collective_id=0, has_side_effects=True, vmem_limit_bytes=60 << 20
        ),
        cost_estimate=pl.CostEstimate(
            flops=6 * count * BS * BS * width, bytes_accessed=4 * count * BS * BS, transcendentals=0
        ),
    )(
        users.reshape(own_u, width),
        items.reshape(own_i, width),
        block_user.reshape(1, count),
        block_item.reshape(1, count),
        ratings.reshape(count, BS, BS),
        weights.reshape(count, BS, BS),
    )
    return (new_users.reshape(users.shape), new_items.reshape(items.shape))


def solution(mesh):
    sizes = dict(mesh.shape)
    return jax.shard_map(
        functools.partial(shards, sizes["row"], sizes["col"]),
        mesh=mesh,
        in_specs=(
            P("row", "col", None),
            P("row", "col", None),
            P("row", "col", None),
            P("row", "col", None),
            P("row", "col", None, None, None),
            P("row", "col", None, None, None),
        ),
        out_specs=(P("row", "col", None), P("row", "col", None)),
        check_vma=False,
    )
```

```python
import functools

import jax
import jax.numpy as jnp
from jax import lax
from jax.experimental import pallas as pl
from jax.experimental.pallas import tpu as pltpu
from jax.sharding import PartitionSpec as P

BS = 128
GROUP = 16
MESH = pl.DeviceIdType.MESH
NT = (((1,), (1,)), ((), ()))
NN = (((1,), (0,)), ((), ()))
TN = (((0,), (0,)), ((), ()))


def dot(a, b, dims):
    return lax.dot_general(a, b, dims, preferred_element_type=jnp.float32)


def chain_tables(key_ref, pad_ref, count):
    pad_ref[...] = jnp.full((8, 128), -1, jnp.int32)
    pad_ref[0:1, 0:count] = key_ref[...]
    across = jnp.broadcast_to(pad_ref[0:1, :], (128, 128))
    down = across.T
    i = lax.broadcasted_iota(jnp.int32, (128, 128), 0)
    j = lax.broadcasted_iota(jnp.int32, (128, 128), 1)
    prev = jnp.max(jnp.where((down == across) & (i < j), i + 1, 0), axis=0, keepdims=True)
    last = jnp.max(jnp.where(down == j, i + 1, 0), axis=0, keepdims=True)
    return prev, last, jnp.maximum(pad_ref[0:1, :], 0)


def spots(index, own):
    if own >= BS:
        blocks = own // BS
        return [(index * blocks + k, 0, BS) for k in range(blocks)]
    per = BS // own
    return [(lax.div(index, per), lax.rem(index, per) * own, own)]


def part(block, first, rows, turn_ref):
    if rows == BS:
        return block
    turn_ref[...] = block
    return turn_ref[pl.ds(pl.multiple_of(first, rows), rows), :]


def owned(slab_ref, index, own):
    if own >= BS:
        return slab_ref.at[pl.ds(index * (own // BS), own // BS)]
    per = BS // own
    return slab_ref.at[lax.div(index, per), pl.ds(pl.multiple_of(lax.rem(index, per) * own, own), own)]


def weight_tile(wseg_ref, slots):
    row = lax.broadcasted_iota(jnp.int32, (8, 128), 0)
    tile = jnp.zeros((8, 128), jnp.float32)
    for k, slot in enumerate(slots):
        tile = jnp.where(row == k, wseg_ref[slot], tile)
    return tile


def weight_sums(ref, place, own):
    both = ref[place, own : own + 16, :].astype(jnp.float32)
    return both[0:8] + both[8:16]


def pack(seg_ref, wseg_ref, tab, line, index, own, out_ref, place, turn_ref, held_ref=None, held=None):
    pieces = spots(index, own)
    slots = [tab[line, block] for block, _, _ in pieces]
    for k, (slot, (_, first, rows)) in enumerate(zip(slots, pieces)):
        at = slice(k * BS, k * BS + rows)
        sums = part(seg_ref[slot], first, rows, turn_ref)
        if held_ref is not None:
            sums = sums + held_ref[held, at, :].astype(jnp.float32)
        out_ref[place, at, :] = sums.astype(jnp.bfloat16)
    tile = weight_tile(wseg_ref, slots)
    if held_ref is not None:
        tile = tile + weight_sums(held_ref, held, own)
    high = tile.astype(jnp.bfloat16).astype(jnp.float32)
    both = jnp.concatenate([high, tile - high], axis=0)
    out_ref[place, own : own + 16, :] = both.astype(jnp.bfloat16)


def update(old_ref, seg_ref, wseg_ref, tab, line, index, own, terms, acc_ref, turn_ref, new_ref):
    pieces = spots(index, own)
    slots = [tab[line, block] for block, _, _ in pieces]
    for k, (slot, (_, first, rows)) in enumerate(zip(slots, pieces)):
        acc_ref[k * BS : k * BS + rows, :] = part(seg_ref[slot], first, rows, turn_ref)
    tile = weight_tile(wseg_ref, slots)
    for wait, recv_ref, place in terms:
        wait()
        acc_ref[...] += recv_ref[place, 0:own, :].astype(jnp.float32)
        tile = tile + weight_sums(recv_ref, place, own)
    for k, (_, first, rows) in enumerate(pieces):
        turned = jnp.broadcast_to(tile[k : k + 1, :], (BS, BS)).T
        turned = part(turned, first, rows, turn_ref)
        at = slice(k * BS, k * BS + rows)
        old = old_ref[at, :]
        new_ref[at, :] = old - 2.0 * (acc_ref[at, :] + 0.5 * old) / (1.0 + turned)


def kernel(
    n_row, n_col, count, own_u, own_i,
    users_hbm, items_hbm, bu_hbm, bi_hbm, ratings, weights,
    new_users, new_items,
    users, items, bu, bi,
    slab_u, slab_i, rat, wts, resid, seg_u, seg_i, wseg_u, wseg_i,
    send_u, send_t, send_i, recv_u, recv_t, recv_i, acc_u, acc_i, turn, pad, tab_v, tab,
    load_sem, gu_send, gu_recv, gi_send, gi_recv, gf_send, gf_recv,
    ru_send, ru_recv, rt_send, rt_recv, ri_send, ri_recv,
):
    row, col = lax.axis_index("row"), lax.axis_index("col")
    col_peers = [lax.rem(col + d, n_col) for d in range(1, n_col)]
    twin = row + 1 - 2 * lax.rem(row, 2)
    half = n_row // 2
    row_peers = [lax.rem(row + 2 * d, n_row) for d in range(1, half)]

    barrier = pltpu.get_barrier_semaphore()
    for peer in col_peers:
        pl.semaphore_signal(barrier, inc=1, device_id=(row, peer), device_id_type=MESH)
    for peer in row_peers + [twin]:
        pl.semaphore_signal(barrier, inc=1, device_id=(peer, col), device_id_type=MESH)
    sources = (users_hbm, items_hbm, bu_hbm, bi_hbm, weights, ratings)
    loads = [
        pltpu.make_async_copy(source, place, load_sem.at[k])
        for k, (source, place) in enumerate(zip(sources, (users, items, bu, bi, wts, rat)))
    ]
    for load in loads:
        load.start()
    load_wts, load_rat = loads[4:]
    for load in loads[:4]:
        load.wait()
    mine_u, mine_i = owned(slab_u, col, own_u), owned(slab_i, row, own_i)
    mine_u[...] = users[...].astype(jnp.bfloat16).reshape(mine_u.shape)
    mine_i[...] = items[...].astype(jnp.bfloat16).reshape(mine_i.shape)
    pl.semaphore_wait(barrier, n_col + half - 1)

    gathers = []
    for place, peer in enumerate(col_peers):
        gathers.append(pltpu.make_async_remote_copy(
            src_ref=mine_u, dst_ref=mine_u,
            send_sem=gu_send.at[place], recv_sem=gu_recv.at[place],
            device_id=(row, peer), device_id_type=MESH))
    for place, peer in enumerate(row_peers + [twin]):
        gathers.append(pltpu.make_async_remote_copy(
            src_ref=mine_i, dst_ref=mine_i,
            send_sem=gi_send.at[place], recv_sem=gi_recv.at[place],
            device_id=(peer, col), device_id_type=MESH))
    for copy in gathers:
        copy.start()

    prev_u, last_u, key_u = chain_tables(bu, pad, count)
    prev_i, last_i, key_i = chain_tables(bi, pad, count)
    for line, values in enumerate((prev_u, prev_i, last_u, last_i, key_u, key_i)):
        tab_v[line : line + 1, :] = values
    to_scalar = pltpu.make_async_copy(tab_v, tab, load_sem.at[6])
    to_scalar.start()
    seg_u[0] = jnp.zeros((BS, BS), jnp.float32)
    seg_i[0] = jnp.zeros((BS, BS), jnp.float32)
    wseg_u[0] = jnp.zeros((8, BS), jnp.float32)
    wseg_i[0] = jnp.zeros((8, BS), jnp.float32)
    to_scalar.wait()
    load_wts.wait()

    ones = jnp.ones((8, BS), jnp.bfloat16)

    def weight_step(b, carry):
        w = wts[b]
        wseg_u[b + 1] = wseg_u[tab[0, b]] + dot(ones, w, NT)
        wseg_i[b + 1] = wseg_i[tab[1, b]] + dot(ones, w, NN)
        return carry

    lax.fori_loop(0, count, weight_step, 0, unroll=4)

    load_rat.wait()
    forwards = []
    for place in range(half - 1):
        gathers[n_col - 1 + place].wait_recv()
        block = owned(slab_i, lax.rem(row + n_row - 2 * (place + 1), n_row), own_i)
        copy = pltpu.make_async_remote_copy(
            src_ref=block, dst_ref=block, send_sem=gf_send.at[place], recv_sem=gf_recv.at[place],
            device_id=(twin, col), device_id_type=MESH)
        copy.start()
        forwards.append(copy)
    for k, copy in enumerate(gathers):
        copy.wait_send()
        if k < n_col - 1 or k == len(gathers) - 1:
            copy.wait_recv()
    for copy in forwards:
        copy.wait()

    group = GROUP if count % GROUP == 0 else 1

    def user_step(g, carry):
        blocks = [g * group + k for k in range(group)]
        us = [slab_u[tab[4, b]] for b in blocks]
        vs = [slab_i[tab[5, b]] for b in blocks]
        preds = [dot(u, v, NT) for u, v in zip(us, vs)]
        rs = [
            (wts[b].astype(jnp.float32) * (pred - rat[b].astype(jnp.float32))).astype(jnp.bfloat16)
            for b, pred in zip(blocks, preds)
        ]
        grads = [dot(r, v, NN) for r, v in zip(rs, vs)]
        for b, r in zip(blocks, rs):
            resid[b] = r
        for b, grad in zip(blocks, grads):
            seg_u[b + 1] = seg_u[tab[0, b]] + grad
        return carry

    lax.fori_loop(0, count // group, user_step, 0)

    sends_u = []
    for place, peer in enumerate(col_peers):
        pack(seg_u, wseg_u, tab, 2, peer, own_u, send_u, place, turn)
        copy = pltpu.make_async_remote_copy(
            src_ref=send_u.at[place], dst_ref=recv_u.at[place],
            send_sem=ru_send.at[place], recv_sem=ru_recv.at[place],
            device_id=(row, peer), device_id_type=MESH)
        copy.start()
        sends_u.append(copy)

    def item_step(g, carry):
        blocks = [g * group + k for k in range(group)]
        grads = [dot(resid[b], slab_u[tab[4, b]], TN) for b in blocks]
        for b, grad in zip(blocks, grads):
            seg_i[b + 1] = seg_i[tab[1, b]] + grad
        return carry

    lax.fori_loop(0, count // group, item_step, 0)

    to_twin = []
    for place in list(range(1, half)) + [0]:
        pack(seg_i, wseg_i, tab, 3, lax.rem(twin + 2 * place, n_row), own_i, send_t, place, turn)
        copy = pltpu.make_async_remote_copy(
            src_ref=send_t.at[place], dst_ref=recv_t.at[place],
            send_sem=rt_send.at[place], recv_sem=rt_recv.at[place],
            device_id=(twin, col), device_id_type=MESH)
        copy.start()
        to_twin.append(copy)

    sends_i = []
    for place, peer in enumerate(row_peers):
        to_twin[place].wait_recv()
        pack(seg_i, wseg_i, tab, 3, peer, own_i, send_i, place, turn, recv_t, place + 1)
        copy = pltpu.make_async_remote_copy(
            src_ref=send_i.at[place], dst_ref=recv_i.at[place],
            send_sem=ri_send.at[place], recv_sem=ri_recv.at[place],
            device_id=(peer, col), device_id_type=MESH)
        copy.start()
        sends_i.append(copy)

    terms_u = [(c.wait_recv, recv_u, k) for k, c in enumerate(sends_u)]
    terms_i = [(to_twin[-1].wait_recv, recv_t, 0)] + [(c.wait_recv, recv_i, k) for k, c in enumerate(sends_i)]
    update(users, seg_u, wseg_u, tab, 2, col, own_u, terms_u, acc_u, turn, new_users)
    update(items, seg_i, wseg_i, tab, 3, row, own_i, terms_i, acc_i, turn, new_items)
    for copy in sends_u + to_twin + sends_i:
        copy.wait_send()


def shards(n_row, n_col, users, items, block_user, block_item, ratings, weights):
    own_u, own_i = users.shape[1], items.shape[0]
    width = users.shape[2]
    count = block_user.shape[2]
    half = n_row // 2
    all_u, all_i = own_u * n_col, own_i * n_row
    vmem = pl.BlockSpec(memory_space=pltpu.VMEM)
    hbm = pl.BlockSpec(memory_space=pltpu.HBM)
    bf16, f32, i32 = jnp.bfloat16, jnp.float32, jnp.int32
    dma = pltpu.SemaphoreType.DMA
    new_users, new_items = pl.pallas_call(
        functools.partial(kernel, n_row, n_col, count, own_u, own_i),
        out_shape=(
            pltpu.VMEM((own_u, width), f32),
            pltpu.VMEM((own_i, width), f32),
        ),
        in_specs=[hbm] * 6,
        out_specs=(vmem, vmem),
        scratch_shapes=[
            pltpu.VMEM((own_u, width), f32),
            pltpu.VMEM((own_i, width), f32),
            pltpu.VMEM((1, count), i32),
            pltpu.VMEM((1, count), i32),
            pltpu.VMEM((all_u // BS, BS, width), bf16),
            pltpu.VMEM((all_i // BS, BS, width), bf16),
            pltpu.VMEM((count, BS, BS), bf16),
            pltpu.VMEM((count, BS, BS), bf16),
            pltpu.VMEM((count, BS, BS), bf16),
            pltpu.VMEM((count + 1, BS, width), f32),
            pltpu.VMEM((count + 1, BS, width), f32),
            pltpu.VMEM((count + 1, 8, BS), f32),
            pltpu.VMEM((count + 1, 8, BS), f32),
            pltpu.VMEM((n_col - 1, own_u + 16, width), bf16),
            pltpu.VMEM((half, own_i + 16, width), bf16),
            pltpu.VMEM((half - 1, own_i + 16, width), bf16),
            pltpu.VMEM((n_col - 1, own_u + 16, width), bf16),
            pltpu.VMEM((half, own_i + 16, width), bf16),
            pltpu.VMEM((half - 1, own_i + 16, width), bf16),
            pltpu.VMEM((own_u, width), f32),
            pltpu.VMEM((own_i, width), f32),
            pltpu.VMEM((BS, BS), f32),
            pltpu.VMEM((8, 128), i32),
            pltpu.VMEM((8, 128), i32),
            pltpu.SMEM((8, 128), i32),
            dma((7,)),
            dma((n_col - 1,)),
            dma((n_col - 1,)),
            dma((half,)),
            dma((half,)),
            dma((half - 1,)),
            dma((half - 1,)),
            dma((n_col - 1,)),
            dma((n_col - 1,)),
            dma((half,)),
            dma((half,)),
            dma((half - 1,)),
            dma((half - 1,)),
        ],
        compiler_params=pltpu.CompilerParams(
            collective_id=0, has_side_effects=True, vmem_limit_bytes=60 << 20
        ),
        cost_estimate=pl.CostEstimate(
            flops=6 * count * BS * BS * width, bytes_accessed=4 * count * BS * BS, transcendentals=0
        ),
    )(
        users.reshape(own_u, width),
        items.reshape(own_i, width),
        block_user.reshape(1, count),
        block_item.reshape(1, count),
        ratings.reshape(count, BS, BS),
        weights.reshape(count, BS, BS),
    )
    return (new_users.reshape(users.shape), new_items.reshape(items.shape))


def solution(mesh):
    sizes = dict(mesh.shape)
    return jax.shard_map(
        functools.partial(shards, sizes["row"], sizes["col"]),
        mesh=mesh,
        in_specs=(
            P("row", "col", None),
            P("row", "col", None),
            P("row", "col", None),
            P("row", "col", None),
            P("row", "col", None, None, None),
            P("row", "col", None, None, None),
        ),
        out_specs=(P("row", "col", None), P("row", "col", None)),
        check_vma=False,
    )
```

```python
import functools

import jax
import jax.numpy as jnp
from jax import lax
from jax.experimental import pallas as pl
from jax.experimental.pallas import tpu as pltpu
from jax.sharding import PartitionSpec as P

BS = 128
GROUP = 24
MESH = pl.DeviceIdType.MESH
NT = (((1,), (1,)), ((), ()))
NN = (((1,), (0,)), ((), ()))
TN = (((0,), (0,)), ((), ()))


def dot(a, b, dims):
    return lax.dot_general(a, b, dims, preferred_element_type=jnp.float32)


def chain_tables(key_ref, pad_ref, count):
    pad_ref[...] = jnp.full((8, 128), -1, jnp.int32)
    pad_ref[0:1, 0:count] = key_ref[...]
    across = jnp.broadcast_to(pad_ref[0:1, :], (128, 128))
    down = across.T
    i = lax.broadcasted_iota(jnp.int32, (128, 128), 0)
    j = lax.broadcasted_iota(jnp.int32, (128, 128), 1)
    prev = jnp.max(jnp.where((down == across) & (i < j), i + 1, 0), axis=0, keepdims=True)
    last = jnp.max(jnp.where(down == j, i + 1, 0), axis=0, keepdims=True)
    return prev, last, jnp.maximum(pad_ref[0:1, :], 0)


def spots(index, own):
    if own >= BS:
        blocks = own // BS
        return [(index * blocks + k, 0, BS) for k in range(blocks)]
    per = BS // own
    return [(lax.div(index, per), lax.rem(index, per) * own, own)]


def part(block, first, rows, turn_ref):
    if rows == BS:
        return block
    turn_ref[...] = block
    return turn_ref[pl.ds(pl.multiple_of(first, rows), rows), :]


def owned(slab_ref, index, own):
    if own >= BS:
        return slab_ref.at[pl.ds(index * (own // BS), own // BS)]
    per = BS // own
    return slab_ref.at[lax.div(index, per), pl.ds(pl.multiple_of(lax.rem(index, per) * own, own), own)]


def weight_tile(wseg_ref, slots):
    row = lax.broadcasted_iota(jnp.int32, (8, 128), 0)
    tile = jnp.zeros((8, 128), jnp.float32)
    for k, slot in enumerate(slots):
        tile = jnp.where(row == k, wseg_ref[slot], tile)
    return tile


def weight_sums(ref, place, own):
    both = ref[place, own : own + 16, :].astype(jnp.float32)
    return both[0:8] + both[8:16]


def pack(seg_ref, wseg_ref, tab, line, index, own, out_ref, place, turn_ref, held_ref=None, held=None):
    pieces = spots(index, own)
    slots = [tab[line, block] for block, _, _ in pieces]
    for k, (slot, (_, first, rows)) in enumerate(zip(slots, pieces)):
        at = slice(k * BS, k * BS + rows)
        sums = part(seg_ref[slot], first, rows, turn_ref)
        if held_ref is not None:
            sums = sums + held_ref[held, at, :].astype(jnp.float32)
        out_ref[place, at, :] = sums.astype(jnp.bfloat16)
    tile = weight_tile(wseg_ref, slots)
    if held_ref is not None:
        tile = tile + weight_sums(held_ref, held, own)
    high = tile.astype(jnp.bfloat16).astype(jnp.float32)
    both = jnp.concatenate([high, tile - high], axis=0)
    out_ref[place, own : own + 16, :] = both.astype(jnp.bfloat16)


def update(old_ref, seg_ref, wseg_ref, tab, line, index, own, terms, acc_ref, turn_ref, new_ref):
    pieces = spots(index, own)
    slots = [tab[line, block] for block, _, _ in pieces]
    for k, (slot, (_, first, rows)) in enumerate(zip(slots, pieces)):
        acc_ref[k * BS : k * BS + rows, :] = part(seg_ref[slot], first, rows, turn_ref)
    tile = weight_tile(wseg_ref, slots)
    for wait, recv_ref, place in terms:
        wait()
        acc_ref[...] += recv_ref[place, 0:own, :].astype(jnp.float32)
        tile = tile + weight_sums(recv_ref, place, own)
    for k, (_, first, rows) in enumerate(pieces):
        turned = jnp.broadcast_to(tile[k : k + 1, :], (BS, BS)).T
        turned = part(turned, first, rows, turn_ref)
        at = slice(k * BS, k * BS + rows)
        old = old_ref[at, :]
        new_ref[at, :] = old - 2.0 * (acc_ref[at, :] + 0.5 * old) / (1.0 + turned)


def kernel(
    n_row, n_col, count, own_u, own_i,
    users_hbm, items_hbm, bu_hbm, bi_hbm, ratings, weights,
    new_users, new_items,
    users, items, bu, bi,
    slab_u, slab_i, rat, wts, resid, seg_u, seg_i, wseg_u, wseg_i,
    send_u, send_t, send_i, recv_u, recv_t, recv_i, acc_u, acc_i, turn, pad, tab_v, tab,
    load_sem, gu_send, gu_recv, gi_send, gi_recv, gf_send, gf_recv,
    ru_send, ru_recv, rt_send, rt_recv, ri_send, ri_recv,
):
    row, col = lax.axis_index("row"), lax.axis_index("col")
    col_peers = [lax.rem(col + d, n_col) for d in range(1, n_col)]
    twin = row + 1 - 2 * lax.rem(row, 2)
    half = n_row // 2
    row_peers = [lax.rem(row + 2 * d, n_row) for d in range(1, half)]

    barrier = pltpu.get_barrier_semaphore()
    for peer in col_peers:
        pl.semaphore_signal(barrier, inc=1, device_id=(row, peer), device_id_type=MESH)
    for peer in row_peers + [twin]:
        pl.semaphore_signal(barrier, inc=1, device_id=(peer, col), device_id_type=MESH)
    sources = (users_hbm, items_hbm, bu_hbm, bi_hbm, weights, ratings)
    loads = [
        pltpu.make_async_copy(source, place, load_sem.at[k])
        for k, (source, place) in enumerate(zip(sources, (users, items, bu, bi, wts, rat)))
    ]
    for load in loads:
        load.start()
    load_wts, load_rat = loads[4:]
    for load in loads[:4]:
        load.wait()
    mine_u, mine_i = owned(slab_u, col, own_u), owned(slab_i, row, own_i)
    mine_u[...] = users[...].astype(jnp.bfloat16).reshape(mine_u.shape)
    mine_i[...] = items[...].astype(jnp.bfloat16).reshape(mine_i.shape)
    pl.semaphore_wait(barrier, n_col + half - 1)

    gathers = []
    for place, peer in enumerate(col_peers):
        gathers.append(pltpu.make_async_remote_copy(
            src_ref=mine_u, dst_ref=mine_u,
            send_sem=gu_send.at[place], recv_sem=gu_recv.at[place],
            device_id=(row, peer), device_id_type=MESH))
    for place, peer in enumerate(row_peers + [twin]):
        gathers.append(pltpu.make_async_remote_copy(
            src_ref=mine_i, dst_ref=mine_i,
            send_sem=gi_send.at[place], recv_sem=gi_recv.at[place],
            device_id=(peer, col), device_id_type=MESH))
    for copy in gathers[n_col - 1:][::-1] + gathers[:n_col - 1][::-1]:
        copy.start()

    prev_u, last_u, key_u = chain_tables(bu, pad, count)
    prev_i, last_i, key_i = chain_tables(bi, pad, count)
    for line, values in enumerate((prev_u, prev_i, last_u, last_i, key_u, key_i)):
        tab_v[line : line + 1, :] = values
    to_scalar = pltpu.make_async_copy(tab_v, tab, load_sem.at[6])
    to_scalar.start()
    seg_u[0] = jnp.zeros((BS, BS), jnp.float32)
    seg_i[0] = jnp.zeros((BS, BS), jnp.float32)
    wseg_u[0] = jnp.zeros((8, BS), jnp.float32)
    wseg_i[0] = jnp.zeros((8, BS), jnp.float32)
    to_scalar.wait()
    load_wts.wait()

    ones = jnp.ones((8, BS), jnp.bfloat16)

    def weight_step(b, carry):
        w = wts[b]
        wseg_u[b + 1] = wseg_u[tab[0, b]] + dot(ones, w, NT)
        wseg_i[b + 1] = wseg_i[tab[1, b]] + dot(ones, w, NN)
        return carry

    lax.fori_loop(0, count, weight_step, 0, unroll=4)

    load_rat.wait()
    forwards = []
    for place in range(half - 1):
        gathers[n_col - 1 + place].wait_recv()
        block = owned(slab_i, lax.rem(row + n_row - 2 * (place + 1), n_row), own_i)
        copy = pltpu.make_async_remote_copy(
            src_ref=block, dst_ref=block, send_sem=gf_send.at[place], recv_sem=gf_recv.at[place],
            device_id=(twin, col), device_id_type=MESH)
        copy.start()
        forwards.append(copy)
    for k, copy in enumerate(gathers):
        copy.wait_send()
        if k < n_col - 1 or k == len(gathers) - 1:
            copy.wait_recv()
    for copy in forwards:
        copy.wait()

    group = GROUP if count % GROUP == 0 else 1

    def user_step(g, carry):
        blocks = [g * group + k for k in range(group)]
        us = [slab_u[tab[4, b]] for b in blocks]
        vs = [slab_i[tab[5, b]] for b in blocks]
        preds = [dot(u, v, NT) for u, v in zip(us, vs)]
        rs = [
            (wts[b].astype(jnp.float32) * (pred - rat[b].astype(jnp.float32))).astype(jnp.bfloat16)
            for b, pred in zip(blocks, preds)
        ]
        grads = [dot(r, v, NN) for r, v in zip(rs, vs)]
        for b, r in zip(blocks, rs):
            resid[b] = r
        for b, grad in zip(blocks, grads):
            seg_u[b + 1] = seg_u[tab[0, b]] + grad
        return carry

    lax.fori_loop(0, count // group, user_step, 0)

    sends_u = []
    for place, peer in enumerate(col_peers):
        pack(seg_u, wseg_u, tab, 2, peer, own_u, send_u, place, turn)
        copy = pltpu.make_async_remote_copy(
            src_ref=send_u.at[place], dst_ref=recv_u.at[place],
            send_sem=ru_send.at[place], recv_sem=ru_recv.at[place],
            device_id=(row, peer), device_id_type=MESH)
        copy.start()
        sends_u.append(copy)

    def item_step(g, carry):
        blocks = [g * group + k for k in range(group)]
        grads = [dot(resid[b], slab_u[tab[4, b]], TN) for b in blocks]
        for b, grad in zip(blocks, grads):
            seg_i[b + 1] = seg_i[tab[1, b]] + grad
        return carry

    lax.fori_loop(0, count // group, item_step, 0)

    to_twin = []
    for place in list(range(1, half)) + [0]:
        pack(seg_i, wseg_i, tab, 3, lax.rem(twin + 2 * place, n_row), own_i, send_t, place, turn)
        copy = pltpu.make_async_remote_copy(
            src_ref=send_t.at[place], dst_ref=recv_t.at[place],
            send_sem=rt_send.at[place], recv_sem=rt_recv.at[place],
            device_id=(twin, col), device_id_type=MESH)
        copy.start()
        to_twin.append(copy)

    sends_i = []
    for place, peer in enumerate(row_peers):
        to_twin[place].wait_recv()
        pack(seg_i, wseg_i, tab, 3, peer, own_i, send_i, place, turn, recv_t, place + 1)
        copy = pltpu.make_async_remote_copy(
            src_ref=send_i.at[place], dst_ref=recv_i.at[place],
            send_sem=ri_send.at[place], recv_sem=ri_recv.at[place],
            device_id=(peer, col), device_id_type=MESH)
        copy.start()
        sends_i.append(copy)

    terms_u = [(c.wait_recv, recv_u, k) for k, c in enumerate(sends_u)]
    terms_i = [(to_twin[-1].wait_recv, recv_t, 0)] + [(c.wait_recv, recv_i, k) for k, c in enumerate(sends_i)]
    update(users, seg_u, wseg_u, tab, 2, col, own_u, terms_u, acc_u, turn, new_users)
    update(items, seg_i, wseg_i, tab, 3, row, own_i, terms_i, acc_i, turn, new_items)
    for copy in sends_u + to_twin + sends_i:
        copy.wait_send()


def shards(n_row, n_col, users, items, block_user, block_item, ratings, weights):
    own_u, own_i = users.shape[1], items.shape[0]
    width = users.shape[2]
    count = block_user.shape[2]
    half = n_row // 2
    all_u, all_i = own_u * n_col, own_i * n_row
    vmem = pl.BlockSpec(memory_space=pltpu.VMEM)
    hbm = pl.BlockSpec(memory_space=pltpu.HBM)
    bf16, f32, i32 = jnp.bfloat16, jnp.float32, jnp.int32
    dma = pltpu.SemaphoreType.DMA
    new_users, new_items = pl.pallas_call(
        functools.partial(kernel, n_row, n_col, count, own_u, own_i),
        out_shape=(
            pltpu.VMEM((own_u, width), f32),
            pltpu.VMEM((own_i, width), f32),
        ),
        in_specs=[hbm] * 6,
        out_specs=(vmem, vmem),
        scratch_shapes=[
            pltpu.VMEM((own_u, width), f32),
            pltpu.VMEM((own_i, width), f32),
            pltpu.VMEM((1, count), i32),
            pltpu.VMEM((1, count), i32),
            pltpu.VMEM((all_u // BS, BS, width), bf16),
            pltpu.VMEM((all_i // BS, BS, width), bf16),
            pltpu.VMEM((count, BS, BS), bf16),
            pltpu.VMEM((count, BS, BS), bf16),
            pltpu.VMEM((count, BS, BS), bf16),
            pltpu.VMEM((count + 1, BS, width), f32),
            pltpu.VMEM((count + 1, BS, width), f32),
            pltpu.VMEM((count + 1, 8, BS), f32),
            pltpu.VMEM((count + 1, 8, BS), f32),
            pltpu.VMEM((n_col - 1, own_u + 16, width), bf16),
            pltpu.VMEM((half, own_i + 16, width), bf16),
            pltpu.VMEM((half - 1, own_i + 16, width), bf16),
            pltpu.VMEM((n_col - 1, own_u + 16, width), bf16),
            pltpu.VMEM((half, own_i + 16, width), bf16),
            pltpu.VMEM((half - 1, own_i + 16, width), bf16),
            pltpu.VMEM((own_u, width), f32),
            pltpu.VMEM((own_i, width), f32),
            pltpu.VMEM((BS, BS), f32),
            pltpu.VMEM((8, 128), i32),
            pltpu.VMEM((8, 128), i32),
            pltpu.SMEM((8, 128), i32),
            dma((7,)),
            dma((n_col - 1,)),
            dma((n_col - 1,)),
            dma((half,)),
            dma((half,)),
            dma((half - 1,)),
            dma((half - 1,)),
            dma((n_col - 1,)),
            dma((n_col - 1,)),
            dma((half,)),
            dma((half,)),
            dma((half - 1,)),
            dma((half - 1,)),
        ],
        compiler_params=pltpu.CompilerParams(
            collective_id=0, has_side_effects=True, vmem_limit_bytes=60 << 20
        ),
        cost_estimate=pl.CostEstimate(
            flops=6 * count * BS * BS * width, bytes_accessed=4 * count * BS * BS, transcendentals=0
        ),
    )(
        users.reshape(own_u, width),
        items.reshape(own_i, width),
        block_user.reshape(1, count),
        block_item.reshape(1, count),
        ratings.reshape(count, BS, BS),
        weights.reshape(count, BS, BS),
    )
    return (new_users.reshape(users.shape), new_items.reshape(items.shape))


def solution(mesh):
    sizes = dict(mesh.shape)
    return jax.shard_map(
        functools.partial(shards, sizes["row"], sizes["col"]),
        mesh=mesh,
        in_specs=(
            P("row", "col", None),
            P("row", "col", None),
            P("row", "col", None),
            P("row", "col", None),
            P("row", "col", None, None, None),
            P("row", "col", None, None, None),
        ),
        out_specs=(P("row", "col", None), P("row", "col", None)),
        check_vma=False,
    )
```
